32 devices in a mesh: grp: 2 (over x), tp: 16 (over z, y, core).
Axes of the slice: x: 2, y: 2, z: 4, core: 2. Of those that a mesh axis runs over, the one named last changes fastest.
Arguments:
- queries: bfloat16 [4, 128, 8192], P('grp', None, 'tp'), parts along dimension 0, may hold values from -72 to 72
- kv_cache: bfloat16 [2, 4, 2048, 512], P(None, 'grp'), parts along dimension 1, may hold values from -3 to 3
- span_kv: bfloat16 [2, 4, 128, 512], P(None, 'grp'), parts along dimension 1, may hold values from -4 to 4
- prefix_len: int32 [4], P('grp'), parts along dimension 0, may hold values from 512 to 2048, as said below
- residual: bfloat16 [512, 16384], P(('grp', 'tp')), parts along dimension 0, may hold values from -1.1953125 to 1.1953125
- out_weight: bfloat16 [8192, 16384], P('tp'), may hold values from -0.0625 to 0.0625
- sign_bits: int32 [16384], replicated, may hold values from 0 to 1
Outputs:
- stream: bfloat16 [512, 16384], P(('grp', 'tp')), parts along dimension 0
- normed: bfloat16 [512, 16384], P('grp'), parts along dimension 0
The draws below stay inside these ranges and needn't reach their ends.
There are 2 independent parts, one for each index of `grp`. The reference program is written for one: setup_inputs(seed, part) draws one part's arguments, and reference() takes and returns one part's arrays. A program takes and returns all parts, laid end to end along the dimension named above; an argument that names none is the same for every part. Nothing has to cross between parts.
Inputs may be any that keep to these rules, and one draw needn't show every extreme that they name: `prefix_len`: some sequence has all 2048 positions in use in every draw.
All inputs are finite; a program needn't handle non-finite values.
Results may differ from the reference program's by a relative error of at most 0.0064.
Values may be sent and summed in bfloat16 or wider, within the bound.
A program may use at most 192 MiB of HBM per device.

```python
import math
import jax
import jax.numpy as jnp
from jax import lax

D = 16384
H = 64
KVH = 4
HD = 128
HB = 256
SPAN = 128
SEQS = 2
PREFIX = 2048
ROWS = 256
N_TP = 16


def cache_values(key):
    drawn = jax.random.normal(jax.random.fold_in(key, 77), (2, SEQS, PREFIX, KVH * HD), jnp.float32)
    return jnp.clip(drawn, -3.0, 3.0)


def draw_kv_cache(key, part):
    drawn = cache_values(key)
    return drawn.astype(jnp.bfloat16)


def draw_queries(key, part):
    key = jax.random.fold_in(key, 2)
    queries_raw = 2.0 * jnp.clip(jax.random.normal(key, (SEQS, SPAN, H, HD), jnp.float32), -3.0, 3.0)
    return queries_raw.reshape(SEQS, SPAN, H * HD).astype(jnp.bfloat16)


def draw_prefix_len(key, part):
    key = jax.random.fold_in(key, 3)
    key_lengths, key_pick = jax.random.split(key)
    lengths = jax.random.randint(key_lengths, (SEQS,), PREFIX // 4, PREFIX + 1)
    picked = jax.random.randint(key_pick, (), 0, SEQS)
    return jnp.where(jnp.arange(SEQS) == picked, PREFIX, lengths).astype(jnp.int32)


def set_ends(values, rng, low, high):
    shape = values.shape
    place = [jax.random.randint(jax.random.fold_in(rng, axis), (), 0, shape[axis]) for axis in range(len(shape))]
    values = values.at[tuple(place)].set(low)
    longest = shape.index(max(shape))
    place[longest] = (place[longest] + 1) % shape[longest]
    return values.at[tuple(place)].set(high)


def block_scale(key, shape, pieces, least, high):
    def one(dim, shards_of):
        heights = jax.random.uniform(jax.random.fold_in(jax.random.fold_in(key, 6), dim), (shards_of,), jnp.float32, least / len(pieces), high / len(pieces))
        return jnp.repeat(jnp.exp(heights), shape[dim] // shards_of).reshape((-1,) + (1,) * (len(shape) - dim - 1))

    loudness = one(*pieces[0])
    for cut in pieces[1:]:
        loudness = loudness * one(*cut)
    return loudness


def bell_draw(rng, shape, width, limit, pieces=(), held_as=jnp.bfloat16):
    factor_of = block_scale(rng, shape, pieces, -0.22, 0.18) if pieces else 1.0
    values = jax.random.normal(rng, shape, jnp.float32) * width * factor_of
    return jnp.minimum(jnp.maximum(values, -limit), limit).astype(held_as)


def setup_inputs(seed: int = 0, part: int = 0) -> dict:
    seeds = jax.random.split(jax.random.key(seed), 8)
    part_keys = jax.random.split(jax.random.fold_in(seeds[7], part), 8)
    return {
        "queries": draw_queries(jax.random.fold_in(jax.random.fold_in(seeds[7], part), 71), part),
        "kv_cache": draw_kv_cache(jax.random.fold_in(jax.random.fold_in(seeds[7], part), 71), part),
        "span_kv": bell_draw(part_keys[2], (2, SEQS, SPAN, KVH * HD), 1.0, 4.0),
        "prefix_len": draw_prefix_len(jax.random.fold_in(jax.random.fold_in(seeds[7], part), 71), part),
        "residual": bell_draw(part_keys[4], (ROWS, D), 0.2, 1.1953125, ((0, 16),)),
        "out_weight": bell_draw(seeds[5], (H * HD, D), (H * HD) ** -0.5, 0.0625, ((0, 16),)),
        "sign_bits": set_ends(jax.random.randint(seeds[6], (D,), 0, 2), jax.random.fold_in(seeds[6], 1), 0, 1).astype(jnp.int32),
    }


def hadamard(size):
    indices = jnp.arange(size, dtype=jnp.int32)
    common = indices[:, None] & indices[None, :]
    parity = jnp.zeros((size, size), jnp.int32)
    for position in range(size.bit_length() - 1):
        parity = parity + (common >> position & 1)
    return (1 - 2 * (parity % 2)).astype(jnp.float32) / math.sqrt(size)

def rotate_rows(values, sign_values, hadamard_table):
    rows_here, columns = values.shape
    block_len = hadamard_table.shape[0]
    rotated = (values * sign_values).reshape(rows_here, columns // block_len, block_len)
    rotated = jnp.einsum('rkb,bc->rkc', rotated, hadamard_table, precision=lax.Precision.HIGHEST)
    return rotated.reshape(rows_here, columns)

def reference(queries, kv_cache, span_kv, prefix_len, residual, out_weight, sign_bits):
    group_size = H // KVH
    keys_all = jnp.concatenate([kv_cache[0], span_kv[0]], axis=1)
    values_all = jnp.concatenate([kv_cache[1], span_kv[1]], axis=1)
    positions = jnp.arange(PREFIX + SPAN, dtype=jnp.int32)
    query_pos = jnp.arange(SPAN, dtype=jnp.int32)
    visible = jnp.where(positions[None, None, :] < PREFIX, positions[None, None, :] < prefix_len[:, None, None], positions[None, None, :] - PREFIX <= query_pos[None, :, None])

    def one_head(head):
        kv_head = head // group_size
        query_cols = lax.dynamic_slice_in_dim(queries, (head * HD).astype(jnp.int32), HD, 2).astype(jnp.float32)
        key_cols = lax.dynamic_slice_in_dim(keys_all, (kv_head * HD).astype(jnp.int32), HD, 2).astype(jnp.float32)
        value_cols = lax.dynamic_slice_in_dim(values_all, (kv_head * HD).astype(jnp.int32), HD, 2).astype(jnp.float32)
        scores = jnp.einsum('btd,bjd->btj', query_cols, key_cols) / math.sqrt(HD)
        scores = jnp.where(visible, scores, -1e+30)
        largest = lax.optimization_barrier(jnp.max(scores, axis=-1, keepdims=True))
        powered = jnp.where(visible, jnp.exp(scores - largest), 0.0)
        weights = (powered / lax.optimization_barrier(jnp.sum(powered, axis=-1, keepdims=True))).astype(jnp.bfloat16)
        return jnp.einsum('btj,bjd->btd', weights.astype(jnp.float32), value_cols).astype(jnp.bfloat16)
    per_head = lax.map(one_head, jnp.arange(H, dtype=jnp.int32))
    attended = per_head.transpose(1, 2, 0, 3).reshape(SEQS * SPAN, H * HD)
    hadamard_table = hadamard(HB)
    sign_values = (2 * sign_bits - 1).astype(jnp.float32)
    cols_shard = H * HD // N_TP

    def add_shard(reduced, shard):
        first_col = (shard * cols_shard).astype(jnp.int32)
        rows_block = lax.dynamic_slice_in_dim(attended, first_col, cols_shard, 1)
        weight_rows = lax.dynamic_slice_in_dim(out_weight, first_col, cols_shard, 0)
        partial_value = jnp.dot(rows_block, weight_rows, preferred_element_type=jnp.float32).astype(jnp.bfloat16)
        partial_value = lax.optimization_barrier(partial_value)
        return (reduced + partial_value.astype(jnp.float32), None)
    reduced, unused = lax.scan(add_shard, jnp.zeros((SEQS * SPAN, D), jnp.float32), jnp.arange(N_TP, dtype=jnp.int32))
    rotated = rotate_rows(reduced, sign_values, hadamard_table)
    stream = (residual.astype(jnp.float32) + rotated).astype(jnp.bfloat16)
    stream_wide = lax.optimization_barrier(stream).astype(jnp.float32)
    normed = (stream_wide * lax.rsqrt(lax.optimization_barrier(jnp.mean(stream_wide * stream_wide, axis=-1, keepdims=True)) + 1e-05)).astype(jnp.bfloat16)
    return (stream, normed)
```

```python
import functools
import math

import jax
import jax.numpy as jnp
from jax import lax
from jax.experimental import pallas as pl
from jax.experimental.pallas import tpu as pltpu
from jax.sharding import PartitionSpec as P

H = 64
KVH = 4
HD = 128
HB = 256
CHUNK = 1024
MIB = 1 << 20


def hadamard(size):
    indices = jnp.arange(size, dtype=jnp.int32)
    common = indices[:, None] & indices[None, :]
    parity = jnp.zeros((size, size), jnp.int32)
    for position in range(size.bit_length() - 1):
        parity = parity + (common >> position & 1)
    return (1 - 2 * (parity % 2)).astype(jnp.float32) / math.sqrt(size)


def attention_kernel(scalars, q_ref, cache_ref, span_ref, out_ref):
    seq = pl.program_id(0)
    length = scalars[1 + seq]
    prefix_cap = cache_ref.shape[2]
    span = span_ref.shape[2]
    _, _, z_here, rows, local_cols = out_ref.shape
    scale = math.log2(math.e) / math.sqrt(HD)
    keys, values = cache_ref[0, 0], cache_ref[1, 0]
    span_keys, span_values = span_ref[0, 0], span_ref[1, 0]
    trans = (((1,), (1,)), ((), ()))
    shown = lax.broadcasted_iota(jnp.int32, (span, prefix_cap), 1) < length
    token = lax.broadcasted_iota(jnp.int32, (span, span), 0)
    causal = lax.broadcasted_iota(jnp.int32, (span, span), 1) <= token
    for head in range(local_cols // HD):
        at = slice(head * HD, (head + 1) * HD)
        q = q_ref[0, :, at]
        s0 = lax.dot_general(q, keys, trans, preferred_element_type=jnp.float32)
        s1 = lax.dot_general(q, span_keys, trans, preferred_element_type=jnp.float32)
        s0 = jnp.where(shown, s0, -1e30)
        s1 = jnp.where(causal, s1, -1e30)
        top = jnp.maximum(jnp.max(s0, axis=1, keepdims=True), jnp.max(s1, axis=1, keepdims=True))
        p0 = jnp.exp2((s0 - top) * scale)
        p1 = jnp.exp2((s1 - top) * scale)
        total = jnp.sum(p0, axis=1, keepdims=True) + jnp.sum(p1, axis=1, keepdims=True)
        mixed = jnp.dot(p0.astype(jnp.bfloat16), values, preferred_element_type=jnp.float32)
        mixed += jnp.dot(p1.astype(jnp.bfloat16), span_values, preferred_element_type=jnp.float32)
        mixed = (mixed / total).astype(jnp.bfloat16)
        for z in range(z_here):
            for y in range(2):
                for core in range(2):
                    first = ((z * 2 + y) * 2 + core) * rows
                    out_ref[core, y, z, :, at] = mixed[first : first + rows]


def exchange_kernel(
    att_ref, w_ref, res_ref, sign_ref, had_ref, g_ref,
    wbuf, part, got_a, got_b, got_c, own,
    w_sem, own_sem, a_send, a_recv, b_send, b_recv, c_send, c_recv,
    z_send, z_recv, y_send, y_recv, d_send, d_recv,
):
    chunks, z_count, rows, cols = got_b.shape
    me = lax.axis_index("tp")
    core = lax.rem(me, 2)
    y = lax.rem(me // 2, 2)
    z = me // 4
    core_peer = me + 1 - 2 * core
    y_peer = me + 2 - 4 * y

    def z_other(step):
        return lax.rem(z + step, z_count)

    def z_peer(step):
        return z_other(step) * 4 + y * 2 + core

    def at(k):
        return pl.ds(pl.multiple_of(k * cols, cols), cols)

    def remote(src, dst, send, recv, peer):
        return pltpu.make_async_remote_copy(
            src_ref=src, dst_ref=dst, send_sem=send, recv_sem=recv,
            device_id={"tp": peer}, device_id_type=pl.DeviceIdType.MESH,
        )

    def copy_w(k):
        return pltpu.make_async_copy(w_ref.at[:, at(k)], wbuf.at[k], w_sem.at[k])

    def copy_a(k):
        return remote(part.at[k, 1 - core], got_a.at[k], a_send.at[k], a_recv.at[k], core_peer)

    def copy_b(k):
        return remote(part.at[k, core, 1 - y], got_b.at[k], b_send.at[k], b_recv.at[k], y_peer)

    def copy_c(k, step):
        return remote(
            part.at[k, core, y, z_other(step)], got_c.at[k, z],
            c_send.at[k, z_other(step)], c_recv.at[k, z], z_peer(step),
        )

    def arrive_c(k, step):
        there = z_other(step)
        return remote(
            part.at[k, core, y, there], got_c.at[k, there],
            c_send.at[k, there], c_recv.at[k, there], z_peer(step),
        )

    def copy_own(k):
        return pltpu.make_async_copy(own.at[k], g_ref.at[z, y, core, :, at(k)], own_sem.at[k])

    def copy_z(k, step):
        return remote(
            own.at[k], g_ref.at[z, y, core, :, at(k)],
            z_send.at[k, z_other(step)], z_recv.at[k, z], z_peer(step),
        )

    def arrive_z(k, step):
        there = z_other(step)
        return remote(
            own.at[k], g_ref.at[there, y, core, :, at(k)],
            z_send.at[k, there], z_recv.at[k, there], z_peer(step),
        )

    def copy_y(k):
        here = g_ref.at[:, y, core, :, at(k)]
        return remote(here, here, y_send.at[k], y_recv.at[k], y_peer)

    def arrive_y(k):
        here = g_ref.at[:, 1 - y, core, :, at(k)]
        return remote(here, here, y_send.at[k], y_recv.at[k], y_peer)

    def copy_d(k):
        here = g_ref.at[:, :, core, :, at(k)]
        return remote(here, here, d_send.at[k], d_recv.at[k], core_peer)

    def arrive_d(k):
        here = g_ref.at[:, :, 1 - core, :, at(k)]
        return remote(here, here, d_send.at[k], d_recv.at[k], core_peer)

    @pl.loop(0, chunks)
    def _(k):
        copy_w(k).start()

    barrier = pltpu.get_barrier_semaphore()
    peers = [core_peer, y_peer] + [z_peer(step) for step in range(1, z_count)]
    for peer in peers:
        pl.semaphore_signal(
            barrier, inc=1, device_id={"tp": peer}, device_id_type=pl.DeviceIdType.MESH
        )
    pl.semaphore_wait(barrier, len(peers))

    f32 = jnp.float32

    def stage_a(k):
        copy_w(k).wait()
        value = jnp.dot(att_ref[...], wbuf[k], preferred_element_type=f32)
        part[k] = value.astype(jnp.bfloat16).reshape(part.shape[1:])
        copy_a(k).start()

    def stage_b(k):
        copy_a(k).wait_recv()
        for side in range(2):
            part[k, core, side] = (
                part[k, core, side].astype(f32) + got_a[k, side].astype(f32)
            ).astype(jnp.bfloat16)
        copy_b(k).start()

    def stage_c(k):
        copy_b(k).wait_recv()
        part[k, core, y] = (part[k, core, y].astype(f32) + got_b[k].astype(f32)).astype(
            jnp.bfloat16
        )
        for step in range(1, z_count):
            copy_c(k, step).start()

    def stage_z(k):
        total = part[k, core, y, z].astype(f32)
        for step in range(1, z_count):
            arrive_c(k, step).wait_recv()
            total = total + got_c[k, z_other(step)].astype(f32)
        total = total * sign_ref[k]
        blocks = cols // HB
        tall = jnp.concatenate([total[:, i * HB : (i + 1) * HB] for i in range(blocks)], axis=0)
        tall = jnp.dot(
            tall, had_ref[...], precision=lax.Precision.HIGHEST, preferred_element_type=f32
        )
        turned = jnp.concatenate(
            [tall[i * rows : (i + 1) * rows] for i in range(blocks)], axis=1
        )
        own[k] = (res_ref[:, at(k)].astype(f32) + turned).astype(jnp.bfloat16)
        for step in range(1, z_count):
            copy_z(k, step).start()
        copy_own(k).start()

    def stage_y(k):
        copy_own(k).wait()
        for step in range(1, z_count):
            arrive_z(k, step).wait_recv()
        copy_y(k).start()

    def stage_d(k):
        arrive_y(k).wait_recv()
        copy_d(k).start()

    stages = [stage_a, stage_b, stage_c, stage_z, stage_y, stage_d]

    @pl.loop(0, chunks + len(stages) - 1)
    def _(t):
        for lag, stage in enumerate(stages):
            k = t - lag

            @pl.when((k >= 0) & (k < chunks))
            def _():
                stage(k)

    @pl.loop(0, chunks)
    def _(k):
        arrive_d(k).wait_recv()
        copy_a(k).wait_send()
        copy_b(k).wait_send()
        for step in range(1, z_count):
            copy_c(k, step).wait_send()
            copy_z(k, step).wait_send()
        copy_y(k).wait_send()
        copy_d(k).wait_send()


def norm_kernel(scalars, x_ref, stream_ref, normed_ref):
    x = x_ref[...]

    @pl.when(pl.program_id(0) == scalars[0])
    def _():
        stream_ref[...] = x

    wide = x.astype(jnp.float32)
    mean = jnp.mean(wide * wide, axis=-1, keepdims=True)
    normed_ref[...] = (wide * lax.rsqrt(mean + 1e-05)).astype(jnp.bfloat16)


def body(n, queries, kv_cache, span_kv, prefix_len, residual, out_weight, sign_bits):
    me = lax.axis_index("tp")
    seqs, span, local_cols = queries.shape
    prefix_cap = kv_cache.shape[2]
    width = out_weight.shape[1]
    rows = residual.shape[0]
    z_count = n // 4
    kv_head = me * (local_cols // HD) // (H // KVH)
    bf16 = jnp.bfloat16

    attended = pl.pallas_call(
        attention_kernel,
        grid_spec=pltpu.PrefetchScalarGridSpec(
            num_scalar_prefetch=1,
            grid=(seqs,),
            in_specs=[
                pl.BlockSpec((1, span, local_cols), lambda b, s: (b, 0, 0)),
                pl.BlockSpec((2, 1, prefix_cap, HD), lambda b, s: (0, b, 0, s[0])),
                pl.BlockSpec((2, 1, span, HD), lambda b, s: (0, b, 0, s[0])),
            ],
            out_specs=pl.BlockSpec(
                (2, 2, z_count // seqs, rows, local_cols), lambda b, s: (0, 0, b, 0, 0)
            ),
        ),
        out_shape=jax.ShapeDtypeStruct((2, 2, z_count, rows, local_cols), bf16),
        compiler_params=pltpu.CompilerParams(vmem_limit_bytes=40 * MIB),
    )(
        jnp.concatenate([kv_head[None].astype(jnp.int32), prefix_len]),
        queries, kv_cache, span_kv,
    )

    chunks = width // CHUNK
    signs = (2 * sign_bits - 1).astype(jnp.float32).reshape(chunks, 1, CHUNK)
    vmem = pl.BlockSpec(memory_space=pltpu.VMEM)
    hbm = pl.BlockSpec(memory_space=pl.ANY)
    one = pltpu.SemaphoreType.DMA((chunks,))
    per_z = pltpu.SemaphoreType.DMA((chunks, z_count))
    gathered = pl.pallas_call(
        exchange_kernel,
        out_shape=jax.ShapeDtypeStruct((z_count, 2, 2, rows, width), bf16),
        in_specs=[vmem, hbm, vmem, vmem, vmem],
        out_specs=hbm,
        scratch_shapes=[
            pltpu.VMEM((chunks, local_cols, CHUNK), bf16),
            pltpu.VMEM((chunks, 2, 2, z_count, rows, CHUNK), bf16),
            pltpu.VMEM((chunks, 2, z_count, rows, CHUNK), bf16),
            pltpu.VMEM((chunks, z_count, rows, CHUNK), bf16),
            pltpu.VMEM((chunks, z_count, rows, CHUNK), bf16),
            pltpu.VMEM((chunks, rows, CHUNK), bf16),
            one, one, one, one, one, one, per_z, per_z, per_z, per_z, one, one, one, one,
        ],
        compiler_params=pltpu.CompilerParams(
            collective_id=0, has_side_effects=True, vmem_limit_bytes=56 * MIB
        ),
    )(
        attended.reshape(n * rows, local_cols), out_weight, residual, signs, hadamard(HB),
    )
    gathered = gathered.reshape(n * rows, width)

    stream, normed = pl.pallas_call(
        norm_kernel,
        grid_spec=pltpu.PrefetchScalarGridSpec(
            num_scalar_prefetch=1,
            grid=(n,),
            in_specs=[pl.BlockSpec((rows, width), lambda i, s: (i, 0))],
            out_specs=[
                pl.BlockSpec((rows, width), lambda i, s: (0, 0)),
                pl.BlockSpec((rows, width), lambda i, s: (i, 0)),
            ],
        ),
        out_shape=[
            jax.ShapeDtypeStruct((rows, width), bf16),
            jax.ShapeDtypeStruct((n * rows, width), bf16),
        ],
        compiler_params=pltpu.CompilerParams(vmem_limit_bytes=40 * MIB),
    )(me[None].astype(jnp.int32), gathered)
    return (stream, normed)


def solution(mesh):
    in_specs = (
        P("grp", None, "tp"),
        P(None, "grp", None, None),
        P(None, "grp", None, None),
        P("grp"),
        P(("grp", "tp"), None),
        P("tp", None),
        P(),
    )
    out_specs = (P(("grp", "tp"), None), P("grp", None))
    return jax.shard_map(
        functools.partial(body, mesh.shape["tp"]),
        mesh=mesh, in_specs=in_specs, out_specs=out_specs, check_vma=False,
    )
```

```python
import functools
import math

import jax
import jax.numpy as jnp
from jax import lax
from jax.experimental import pallas as pl
from jax.experimental.pallas import tpu as pltpu
from jax.sharding import PartitionSpec as P

H = 64
KVH = 4
HD = 128
HB = 256
CHUNK = 1024
NORM_ROWS = 128
LAGS = (0, 2, 4, 6, 8, 10, 12, 14)
LAGS = (0, 2, 4, 6, 8, 10, 12, 14)
MIB = 1 << 20


def hadamard(size):
    common = lax.broadcasted_iota(jnp.int32, (size, size), 0)
    common = common & lax.broadcasted_iota(jnp.int32, (size, size), 1)
    for shift in (16, 8, 4, 2, 1):
        common = common ^ (common >> shift)
    return (1 - 2 * (common & 1)).astype(jnp.float32) / math.sqrt(size)


def attention_kernel(kv_head, lengths, q_ref, cache_ref, span_ref, out_ref):
    seq = pl.program_id(0)
    length = lengths[seq]
    prefix_cap = cache_ref.shape[2]
    span = span_ref.shape[2]
    _, _, z_here, rows, local_cols = out_ref.shape
    scale = math.log2(math.e) / math.sqrt(HD)
    keys, values = cache_ref[0, 0], cache_ref[1, 0]
    span_keys, span_values = span_ref[0, 0], span_ref[1, 0]
    trans = (((1,), (1,)), ((), ()))
    shown = lax.broadcasted_iota(jnp.int32, (span, prefix_cap), 1) < length
    token = lax.broadcasted_iota(jnp.int32, (span, span), 0)
    causal = lax.broadcasted_iota(jnp.int32, (span, span), 1) <= token
    for head in range(local_cols // HD):
        at = slice(head * HD, (head + 1) * HD)
        q = q_ref[0, :, at]
        s0 = lax.dot_general(q, keys, trans, preferred_element_type=jnp.float32)
        s1 = lax.dot_general(q, span_keys, trans, preferred_element_type=jnp.float32)
        s0 = jnp.where(shown, s0, -1e30)
        s1 = jnp.where(causal, s1, -1e30)
        top = jnp.maximum(jnp.max(s0, axis=1, keepdims=True), jnp.max(s1, axis=1, keepdims=True))
        p0 = jnp.exp2((s0 - top) * scale)
        p1 = jnp.exp2((s1 - top) * scale)
        total = jnp.sum(p0, axis=1, keepdims=True) + jnp.sum(p1, axis=1, keepdims=True)
        mixed = jnp.dot(p0.astype(jnp.bfloat16), values, preferred_element_type=jnp.float32)
        mixed += jnp.dot(p1.astype(jnp.bfloat16), span_values, preferred_element_type=jnp.float32)
        mixed = (mixed / total).astype(jnp.bfloat16)
        for z in range(z_here):
            for y in range(2):
                for core in range(2):
                    first = ((z * 2 + y) * 2 + core) * rows
                    out_ref[core, y, z, :, at] = mixed[first : first + rows]


def exchange_kernel(
    att_ref, w_ref, res_ref, sign_ref, g_ref,
    wbuf, part, got_a, got_b, got_bz, got_c, got_d, own, had_ref,
    w_sem, own_sem, a_send, a_recv, b_send, b_recv, c_send, c_recv, d_send, d_recv,
    e_send, e_recv, f_send, f_recv, g_send, g_recv, h_send, h_recv,
):
    chunks, far_count, rows, cols = got_d.shape
    me = lax.axis_index("tp")
    core = lax.rem(me, 2)
    y = lax.rem(me // 2, 2)
    near = lax.rem(me // 4, 2)
    far = me // 8
    core_peer = me + 1 - 2 * core
    y_peer = me + 2 - 4 * y
    near_peer = me + 4 - 8 * near
    others = range(1, far_count)

    def far_other(step):
        return lax.rem(far + step, far_count)

    def far_peer(step):
        return far_other(step) * 8 + near * 4 + y * 2 + core

    def at(k):
        return pl.ds(pl.multiple_of(k * cols, cols), cols)

    def remote(src, dst, send, recv, peer):
        return pltpu.make_async_remote_copy(
            src_ref=src, dst_ref=dst, send_sem=send, recv_sem=recv,
            device_id={"tp": peer}, device_id_type=pl.DeviceIdType.MESH,
        )

    def by_kind(k, y_first, near_first):
        kind = lax.rem(k, 4)
        pl.when(kind != 1)(y_first)
        pl.when(kind == 1)(near_first)

    def copy_w(k):
        return pltpu.make_async_copy(w_ref.at[:, at(k)], wbuf.at[k], w_sem.at[k])

    def copy_a(k):
        return remote(part.at[k, 1 - core], got_a.at[k], a_send.at[k], a_recv.at[k], core_peer)

    def copy_b_y(k):
        return remote(part.at[k, core, 1 - y], got_b.at[k], b_send.at[k], b_recv.at[k], y_peer)

    def copy_b_near(k):
        return remote(
            part.at[k, core, :, :, 1 - near], got_bz.at[k], b_send.at[k], b_recv.at[k], near_peer
        )

    def copy_c_near(k):
        return remote(
            part.at[k, core, y, :, 1 - near], got_c.at[k], c_send.at[k], c_recv.at[k], near_peer
        )

    def copy_c_y(k):
        return remote(
            part.at[k, core, 1 - y, :, near], got_c.at[k], c_send.at[k], c_recv.at[k], y_peer
        )

    def copy_d(k, step):
        there = far_other(step)
        return remote(
            part.at[k, core, y, there, near], got_d.at[k, far],
            d_send.at[k, there], d_recv.at[k, far], far_peer(step),
        )

    def arrive_d(k, step):
        there = far_other(step)
        return remote(
            part.at[k, core, y, there, near], got_d.at[k, there],
            d_send.at[k, there], d_recv.at[k, there], far_peer(step),
        )

    def copy_own(k):
        return pltpu.make_async_copy(
            own.at[k], g_ref.at[far, near, y, core, :, at(k)], own_sem.at[k]
        )

    def copy_e(k, step):
        return remote(
            own.at[k], g_ref.at[far, near, y, core, :, at(k)],
            e_send.at[k, far_other(step)], e_recv.at[k, far], far_peer(step),
        )

    def arrive_e(k, step):
        there = far_other(step)
        return remote(
            own.at[k], g_ref.at[there, near, y, core, :, at(k)],
            e_send.at[k, there], e_recv.at[k, there], far_peer(step),
        )

    def copy_f(k, near_at, y_at, peer):
        here = g_ref.at[:, near_at, y_at, core, :, at(k)]
        return remote(here, here, f_send.at[k], f_recv.at[k], peer)

    def copy_g_y(k, y_at):
        here = g_ref.at[:, :, y_at, core, :, at(k)]
        return remote(here, here, g_send.at[k], g_recv.at[k], y_peer)

    def copy_g_near(k, near_at):
        here = g_ref.at[:, near_at, :, core, :, at(k)]
        return remote(here, here, g_send.at[k], g_recv.at[k], near_peer)

    def copy_h(k, core_at):
        here = g_ref.at[:, :, :, core_at, :, at(k)]
        return remote(here, here, h_send.at[k], h_recv.at[k], core_peer)

    @pl.loop(0, chunks)
    def _(k):
        copy_w(k).start()

    barrier = pltpu.get_barrier_semaphore()
    peers = [core_peer, y_peer, near_peer] + [far_peer(step) for step in others]
    for peer in peers:
        pl.semaphore_signal(
            barrier, inc=1, device_id={"tp": peer}, device_id_type=pl.DeviceIdType.MESH
        )
    had_ref[...] = hadamard(HB)
    pl.semaphore_wait(barrier, len(peers))

    f32 = jnp.float32

    def plus(left, right):
        return (left.astype(f32) + right.astype(f32)).astype(jnp.bfloat16)

    def stage_a(k):
        copy_w(k).wait()
        value = jnp.dot(att_ref[...], wbuf[k], preferred_element_type=f32)
        part[k] = value.astype(jnp.bfloat16).reshape(part.shape[1:])
        copy_a(k).start()

    def stage_b(k):
        copy_a(k).wait_recv()
        for side in range(2):
            part[k, core, side] = plus(part[k, core, side], got_a[k, side])
        by_kind(k, lambda: copy_b_y(k).start(), lambda: copy_b_near(k).start())

    def stage_c(k):
        def y_first():
            copy_b_y(k).wait_recv()
            part[k, core, y] = plus(part[k, core, y], got_b[k])
            copy_c_near(k).start()

        def near_first():
            copy_b_near(k).wait_recv()
            for side in range(2):
                for block in range(far_count):
                    part[k, core, side, block, near] = plus(
                        part[k, core, side, block, near], got_bz[k, side, block]
                    )
            copy_c_y(k).start()

        by_kind(k, y_first, near_first)

    def stage_d(k):
        by_kind(k, lambda: copy_c_near(k).wait_recv(), lambda: copy_c_y(k).wait_recv())
        for block in range(far_count):
            part[k, core, y, block, near] = plus(
                part[k, core, y, block, near], got_c[k, block]
            )
        for step in others:
            copy_d(k, step).start()

    def stage_e(k):
        total = part[k, core, y, far, near].astype(f32)
        for step in others:
            arrive_d(k, step).wait_recv()
            total = total + got_d[k, far_other(step)].astype(f32)
        total = total * (2 * sign_ref[:, at(k)] - 1).astype(f32)
        blocks = cols // HB
        tall = jnp.concatenate([total[:, i * HB : (i + 1) * HB] for i in range(blocks)], axis=0)
        tall = jnp.dot(
            tall, had_ref[...], precision=lax.Precision.HIGHEST, preferred_element_type=f32
        )
        turned = jnp.concatenate(
            [tall[i * rows : (i + 1) * rows] for i in range(blocks)], axis=1
        )
        own[k] = (res_ref[:, at(k)].astype(f32) + turned).astype(jnp.bfloat16)
        for step in others:
            copy_e(k, step).start()
        copy_own(k).start()

    def stage_f(k):
        copy_own(k).wait()
        for step in others:
            arrive_e(k, step).wait_recv()
        by_kind(
            k,
            lambda: copy_f(k, near, y, near_peer).start(),
            lambda: copy_f(k, near, y, y_peer).start(),
        )

    def stage_g(k):
        def y_last():
            copy_f(k, 1 - near, y, near_peer).wait_recv()
            copy_g_y(k, y).start()

        def near_last():
            copy_f(k, near, 1 - y, y_peer).wait_recv()
            copy_g_near(k, near).start()

        by_kind(k, y_last, near_last)

    def stage_h(k):
        by_kind(
            k,
            lambda: copy_g_y(k, 1 - y).wait_recv(),
            lambda: copy_g_near(k, 1 - near).wait_recv(),
        )
        copy_h(k, core).start()

    stages = [stage_a, stage_b, stage_c, stage_d, stage_e, stage_f, stage_g, stage_h]

    @pl.loop(0, chunks + LAGS[-1])
    def _(t):
        for lag, stage in zip(LAGS, stages):
            k = t - lag

            @pl.when((k >= 0) & (k < chunks))
            def _():
                stage(k)

    @pl.loop(0, chunks)
    def _(k):
        copy_h(k, 1 - core).wait_recv()
        copy_a(k).wait_send()

        def y_kind():
            copy_b_y(k).wait_send()
            copy_c_near(k).wait_send()
            copy_f(k, near, y, near_peer).wait_send()
            copy_g_y(k, y).wait_send()

        def near_kind():
            copy_b_near(k).wait_send()
            copy_c_y(k).wait_send()
            copy_f(k, near, y, y_peer).wait_send()
            copy_g_near(k, near).wait_send()

        by_kind(k, y_kind, near_kind)
        for step in others:
            copy_d(k, step).wait_send()
            copy_e(k, step).wait_send()
        copy_h(k, core).wait_send()


def norm_kernel(scalars, x_ref, stream_ref, normed_ref):
    rows, width = stream_ref.shape
    groups = x_ref.shape[0] // rows
    for group in range(groups):
        here = slice(group * rows, (group + 1) * rows)

        @pl.when(pl.program_id(0) * groups + group == scalars[0])
        def _():
            stream_ref[...] = x_ref[here]

        pieces = [slice(first, first + 1024) for first in range(0, width, 1024)]
        squares = jnp.zeros((rows, 1024), jnp.float32)
        for piece in pieces:
            wide = x_ref[here, piece].astype(jnp.float32)
            squares = squares + wide * wide
        mean = jnp.sum(squares, axis=-1, keepdims=True) / width
        factor = lax.rsqrt(mean + 1e-05)
        for piece in pieces:
            wide = x_ref[here, piece].astype(jnp.float32)
            normed_ref[here, piece] = (wide * factor).astype(jnp.bfloat16)


def body(n, queries, kv_cache, span_kv, prefix_len, residual, out_weight, sign_bits):
    me = lax.axis_index("tp")
    seqs, span, local_cols = queries.shape
    prefix_cap = kv_cache.shape[2]
    width = out_weight.shape[1]
    rows = residual.shape[0]
    z_count, far_count = n // 4, n // 8
    kv_head = me * (local_cols // HD) // (H // KVH)
    bf16 = jnp.bfloat16

    attended = pl.pallas_call(
        attention_kernel,
        grid_spec=pltpu.PrefetchScalarGridSpec(
            num_scalar_prefetch=2,
            grid=(seqs,),
            in_specs=[
                pl.BlockSpec((1, span, local_cols), lambda b, s, _: (b, 0, 0)),
                pl.BlockSpec((2, 1, prefix_cap, HD), lambda b, s, _: (0, b, 0, s[0])),
                pl.BlockSpec((2, 1, span, HD), lambda b, s, _: (0, b, 0, s[0])),
            ],
            out_specs=pl.BlockSpec(
                (2, 2, z_count // seqs, rows, local_cols), lambda b, s, _: (0, 0, b, 0, 0)
            ),
        ),
        out_shape=jax.ShapeDtypeStruct((2, 2, z_count, rows, local_cols), bf16),
        compiler_params=pltpu.CompilerParams(vmem_limit_bytes=60 * MIB),
    )(
        kv_head[None].astype(jnp.int32), prefix_len,
        queries, kv_cache, span_kv,
    )

    chunks = width // CHUNK
    vmem = pl.BlockSpec(memory_space=pltpu.VMEM)
    hbm = pl.BlockSpec(memory_space=pl.ANY)
    one = pltpu.SemaphoreType.DMA((chunks,))
    per_far = pltpu.SemaphoreType.DMA((chunks, far_count))
    gathered = pl.pallas_call(
        exchange_kernel,
        out_shape=jax.ShapeDtypeStruct((far_count, 2, 2, 2, rows, width), bf16),
        in_specs=[vmem, hbm, vmem, vmem],
        out_specs=hbm,
        scratch_shapes=[
            pltpu.VMEM((chunks, local_cols, CHUNK), bf16),
            pltpu.VMEM((chunks, 2, 2, far_count, 2, rows, CHUNK), bf16),
            pltpu.VMEM((chunks, 2, far_count, 2, rows, CHUNK), bf16),
            pltpu.VMEM((chunks, far_count, 2, rows, CHUNK), bf16),
            pltpu.VMEM((chunks, 2, far_count, rows, CHUNK), bf16),
            pltpu.VMEM((chunks, far_count, rows, CHUNK), bf16),
            pltpu.VMEM((chunks, far_count, rows, CHUNK), bf16),
            pltpu.VMEM((chunks, rows, CHUNK), bf16),
            pltpu.VMEM((HB, HB), jnp.float32),
            one, one, one, one, one, one, one, one, per_far, per_far,
            per_far, per_far, one, one, one, one, one, one,
        ],
        compiler_params=pltpu.CompilerParams(
            collective_id=0, has_side_effects=True, vmem_limit_bytes=56 * MIB
        ),
    )(
        attended.reshape(n * rows, local_cols), out_weight, residual, sign_bits[None],
    )
    gathered = gathered.reshape(n * rows, width)

    stream, normed = pl.pallas_call(
        norm_kernel,
        grid_spec=pltpu.PrefetchScalarGridSpec(
            num_scalar_prefetch=1,
            grid=(n * rows // NORM_ROWS,),
            in_specs=[pl.BlockSpec((NORM_ROWS, width), lambda i, s: (i, 0))],
            out_specs=[
                pl.BlockSpec((rows, width), lambda i, s: (0, 0)),
                pl.BlockSpec((NORM_ROWS, width), lambda i, s: (i, 0)),
            ],
        ),
        out_shape=[
            jax.ShapeDtypeStruct((rows, width), bf16),
            jax.ShapeDtypeStruct((n * rows, width), bf16),
        ],
        compiler_params=pltpu.CompilerParams(vmem_limit_bytes=60 * MIB),
    )(me[None].astype(jnp.int32), gathered)
    return (stream, normed)


def solution(mesh):
    in_specs = (
        P("grp", None, "tp"),
        P(None, "grp", None, None),
        P(None, "grp", None, None),
        P("grp"),
        P(("grp", "tp"), None),
        P("tp", None),
        P(),
    )
    out_specs = (P(("grp", "tp"), None), P("grp", None))
    return jax.shard_map(
        functools.partial(body, mesh.shape["tp"]),
        mesh=mesh, in_specs=in_specs, out_specs=out_specs, check_vma=False,
    )
```

```python
import functools
import math

import jax
import jax.numpy as jnp
from jax import lax
from jax.experimental import pallas as pl
from jax.experimental.pallas import tpu as pltpu
from jax.sharding import PartitionSpec as P

H = 64
KVH = 4
HD = 128
HB = 256
CHUNK = 1024
NORM_ROWS = 128
LAGS = (0, 2, 4, 6, 8, 10, 12, 14)
MIB = 1 << 20


def hadamard(size):
    common = lax.broadcasted_iota(jnp.int32, (size, size), 0)
    common = common & lax.broadcasted_iota(jnp.int32, (size, size), 1)
    for shift in (16, 8, 4, 2, 1):
        common = common ^ (common >> shift)
    return (1 - 2 * (common & 1)).astype(jnp.float32) / math.sqrt(size)


def attention_kernel(kv_head, lengths, q_ref, cache_ref, span_ref, out_ref):
    seq = pl.program_id(0)
    length = lengths[seq]
    prefix_cap = cache_ref.shape[2]
    span = span_ref.shape[2]
    _, _, z_here, rows, local_cols = out_ref.shape
    scale = math.log2(math.e) / math.sqrt(HD)
    keys, values = cache_ref[0, 0], cache_ref[1, 0]
    span_keys, span_values = span_ref[0, 0], span_ref[1, 0]
    trans = (((1,), (1,)), ((), ()))
    shown = lax.broadcasted_iota(jnp.int32, (span, prefix_cap), 1) < length
    token = lax.broadcasted_iota(jnp.int32, (span, span), 0)
    causal = lax.broadcasted_iota(jnp.int32, (span, span), 1) <= token
    for head in range(local_cols // HD):
        at = slice(head * HD, (head + 1) * HD)
        q = q_ref[0, :, at]
        s0 = lax.dot_general(q, keys, trans, preferred_element_type=jnp.float32)
        s1 = lax.dot_general(q, span_keys, trans, preferred_element_type=jnp.float32)
        s0 = jnp.where(shown, s0, -1e30)
        s1 = jnp.where(causal, s1, -1e30)
        top = jnp.maximum(jnp.max(s0, axis=1, keepdims=True), jnp.max(s1, axis=1, keepdims=True))
        p0 = jnp.exp2((s0 - top) * scale)
        p1 = jnp.exp2((s1 - top) * scale)
        total = jnp.sum(p0, axis=1, keepdims=True) + jnp.sum(p1, axis=1, keepdims=True)
        mixed = jnp.dot(p0.astype(jnp.bfloat16), values, preferred_element_type=jnp.float32)
        mixed += jnp.dot(p1.astype(jnp.bfloat16), span_values, preferred_element_type=jnp.float32)
        mixed = (mixed / total).astype(jnp.bfloat16)
        for z in range(z_here):
            for y in range(2):
                for core in range(2):
                    first = ((z * 2 + y) * 2 + core) * rows
                    out_ref[core, y, z, :, at] = mixed[first : first + rows]


def exchange_kernel(
    att_ref, w_ref, res_ref, sign_ref, g_ref,
    wbuf, part, got_a, got_b, got_bz, got_c, got_d, own, had_ref,
    w_sem, own_sem, a_send, a_recv, b_send, b_recv, c_send, c_recv, d_send, d_recv,
    e_send, e_recv, f_send, f_recv, g_send, g_recv, h_send, h_recv,
):
    chunks, far_count, rows, cols = got_d.shape
    me = lax.axis_index("tp")
    core = lax.rem(me, 2)
    y = lax.rem(me // 2, 2)
    near = lax.rem(me // 4, 2)
    far = me // 8
    core_peer = me + 1 - 2 * core
    y_peer = me + 2 - 4 * y
    near_peer = me + 4 - 8 * near
    others = range(1, far_count)

    def far_other(step):
        return lax.rem(far + step, far_count)

    def far_peer(step):
        return far_other(step) * 8 + near * 4 + y * 2 + core

    def at(k):
        return pl.ds(pl.multiple_of(k * cols, cols), cols)

    def remote(src, dst, send, recv, peer):
        return pltpu.make_async_remote_copy(
            src_ref=src, dst_ref=dst, send_sem=send, recv_sem=recv,
            device_id={"tp": peer}, device_id_type=pl.DeviceIdType.MESH,
        )

    def by_kind(k, y_first, near_first):
        kind = lax.rem(k, 3)
        pl.when(kind != 1)(y_first)
        pl.when(kind == 1)(near_first)

    def copy_w(k):
        return pltpu.make_async_copy(w_ref.at[:, at(k)], wbuf.at[k], w_sem.at[k])

    def copy_a(k):
        return remote(part.at[k, 1 - core], got_a.at[k], a_send.at[k], a_recv.at[k], core_peer)

    def copy_b_y(k):
        return remote(part.at[k, core, 1 - y], got_b.at[k], b_send.at[k], b_recv.at[k], y_peer)

    def copy_b_near(k):
        return remote(
            part.at[k, core, :, :, 1 - near], got_bz.at[k], b_send.at[k], b_recv.at[k], near_peer
        )

    def copy_c_near(k):
        return remote(
            part.at[k, core, y, :, 1 - near], got_c.at[k], c_send.at[k], c_recv.at[k], near_peer
        )

    def copy_c_y(k):
        return remote(
            part.at[k, core, 1 - y, :, near], got_c.at[k], c_send.at[k], c_recv.at[k], y_peer
        )

    def copy_d(k, step):
        there = far_other(step)
        return remote(
            part.at[k, core, y, there, near], got_d.at[k, far],
            d_send.at[k, there], d_recv.at[k, far], far_peer(step),
        )

    def arrive_d(k, step):
        there = far_other(step)
        return remote(
            part.at[k, core, y, there, near], got_d.at[k, there],
            d_send.at[k, there], d_recv.at[k, there], far_peer(step),
        )

    def copy_own(k):
        return pltpu.make_async_copy(
            own.at[k], g_ref.at[far, near, y, core, :, at(k)], own_sem.at[k]
        )

    def copy_e(k, step):
        return remote(
            own.at[k], g_ref.at[far, near, y, core, :, at(k)],
            e_send.at[k, far_other(step)], e_recv.at[k, far], far_peer(step),
        )

    def arrive_e(k, step):
        there = far_other(step)
        return remote(
            own.at[k], g_ref.at[there, near, y, core, :, at(k)],
            e_send.at[k, there], e_recv.at[k, there], far_peer(step),
        )

    def copy_f(k, near_at, y_at, peer):
        here = g_ref.at[:, near_at, y_at, core, :, at(k)]
        return remote(here, here, f_send.at[k], f_recv.at[k], peer)

    def copy_g_y(k, y_at):
        here = g_ref.at[:, :, y_at, core, :, at(k)]
        return remote(here, here, g_send.at[k], g_recv.at[k], y_peer)

    def copy_g_near(k, near_at):
        here = g_ref.at[:, near_at, :, core, :, at(k)]
        return remote(here, here, g_send.at[k], g_recv.at[k], near_peer)

    def copy_h(k, core_at):
        here = g_ref.at[:, :, :, core_at, :, at(k)]
        return remote(here, here, h_send.at[k], h_recv.at[k], core_peer)

    @pl.loop(0, chunks)
    def _(k):
        copy_w(k).start()

    barrier = pltpu.get_barrier_semaphore()
    peers = [core_peer, y_peer, near_peer] + [far_peer(step) for step in others]
    for peer in peers:
        pl.semaphore_signal(
            barrier, inc=1, device_id={"tp": peer}, device_id_type=pl.DeviceIdType.MESH
        )
    had_ref[...] = hadamard(HB)
    pl.semaphore_wait(barrier, len(peers))

    f32 = jnp.float32

    def plus(left, right):
        return (left.astype(f32) + right.astype(f32)).astype(jnp.bfloat16)

    def stage_a(k):
        copy_w(k).wait()
        value = jnp.dot(att_ref[...], wbuf[k], preferred_element_type=f32)
        part[k] = value.astype(jnp.bfloat16).reshape(part.shape[1:])
        copy_a(k).start()

    def stage_b(k):
        copy_a(k).wait_recv()
        for side in range(2):
            part[k, core, side] = plus(part[k, core, side], got_a[k, side])
        by_kind(k, lambda: copy_b_y(k).start(), lambda: copy_b_near(k).start())

    def stage_c(k):
        def y_first():
            copy_b_y(k).wait_recv()
            part[k, core, y] = plus(part[k, core, y], got_b[k])
            copy_c_near(k).start()

        def near_first():
            copy_b_near(k).wait_recv()
            for side in range(2):
                for block in range(far_count):
                    part[k, core, side, block, near] = plus(
                        part[k, core, side, block, near], got_bz[k, side, block]
                    )
            copy_c_y(k).start()

        by_kind(k, y_first, near_first)

    def stage_d(k):
        by_kind(k, lambda: copy_c_near(k).wait_recv(), lambda: copy_c_y(k).wait_recv())
        for block in range(far_count):
            part[k, core, y, block, near] = plus(
                part[k, core, y, block, near], got_c[k, block]
            )
        for step in others:
            copy_d(k, step).start()

    def stage_e(k):
        total = part[k, core, y, far, near].astype(f32)
        for step in others:
            arrive_d(k, step).wait_recv()
            total = total + got_d[k, far_other(step)].astype(f32)
        total = total * (2 * sign_ref[:, at(k)] - 1).astype(f32)
        blocks = cols // HB
        tall = jnp.concatenate([total[:, i * HB : (i + 1) * HB] for i in range(blocks)], axis=0)
        tall = jnp.dot(
            tall, had_ref[...], precision=lax.Precision.HIGHEST, preferred_element_type=f32
        )
        turned = jnp.concatenate(
            [tall[i * rows : (i + 1) * rows] for i in range(blocks)], axis=1
        )
        own[k] = (res_ref[:, at(k)].astype(f32) + turned).astype(jnp.bfloat16)
        for step in others:
            copy_e(k, step).start()
        copy_own(k).start()

    def stage_f(k):
        copy_own(k).wait()
        for step in others:
            arrive_e(k, step).wait_recv()
        by_kind(
            k,
            lambda: copy_f(k, near, y, near_peer).start(),
            lambda: copy_f(k, near, y, y_peer).start(),
        )

    def stage_g(k):
        def y_last():
            copy_f(k, 1 - near, y, near_peer).wait_recv()
            copy_g_y(k, y).start()

        def near_last():
            copy_f(k, near, 1 - y, y_peer).wait_recv()
            copy_g_near(k, near).start()

        by_kind(k, y_last, near_last)

    def stage_h(k):
        by_kind(
            k,
            lambda: copy_g_y(k, 1 - y).wait_recv(),
            lambda: copy_g_near(k, 1 - near).wait_recv(),
        )
        copy_h(k, core).start()

    stages = [stage_a, stage_b, stage_c, stage_d, stage_e, stage_f, stage_g, stage_h]

    @pl.loop(0, chunks + LAGS[-1])
    def _(t):
        for lag, stage in zip(LAGS, stages):
            k = t - lag

            @pl.when((k >= 0) & (k < chunks))
            def _():
                stage(k)

    @pl.loop(0, chunks)
    def _(k):
        copy_h(k, 1 - core).wait_recv()
        copy_a(k).wait_send()

        def y_kind():
            copy_b_y(k).wait_send()
            copy_c_near(k).wait_send()
            copy_f(k, near, y, near_peer).wait_send()
            copy_g_y(k, y).wait_send()

        def near_kind():
            copy_b_near(k).wait_send()
            copy_c_y(k).wait_send()
            copy_f(k, near, y, y_peer).wait_send()
            copy_g_near(k, near).wait_send()

        by_kind(k, y_kind, near_kind)
        for step in others:
            copy_d(k, step).wait_send()
            copy_e(k, step).wait_send()
        copy_h(k, core).wait_send()


def norm_kernel(scalars, x_ref, stream_ref, normed_ref):
    rows, width = stream_ref.shape
    groups = x_ref.shape[0] // rows
    for group in range(groups):
        here = slice(group * rows, (group + 1) * rows)

        @pl.when(pl.program_id(0) * groups + group == scalars[0])
        def _():
            stream_ref[...] = x_ref[here]

        pieces = [slice(first, first + 1024) for first in range(0, width, 1024)]
        squares = jnp.zeros((rows, 1024), jnp.float32)
        for piece in pieces:
            wide = x_ref[here, piece].astype(jnp.float32)
            squares = squares + wide * wide
        mean = jnp.sum(squares, axis=-1, keepdims=True) / width
        factor = lax.rsqrt(mean + 1e-05)
        for piece in pieces:
            wide = x_ref[here, piece].astype(jnp.float32)
            normed_ref[here, piece] = (wide * factor).astype(jnp.bfloat16)


def body(n, queries, kv_cache, span_kv, prefix_len, residual, out_weight, sign_bits):
    me = lax.axis_index("tp")
    seqs, span, local_cols = queries.shape
    prefix_cap = kv_cache.shape[2]
    width = out_weight.shape[1]
    rows = residual.shape[0]
    z_count, far_count = n // 4, n // 8
    kv_head = me * (local_cols // HD) // (H // KVH)
    bf16 = jnp.bfloat16

    attended = pl.pallas_call(
        attention_kernel,
        grid_spec=pltpu.PrefetchScalarGridSpec(
            num_scalar_prefetch=2,
            grid=(seqs,),
            in_specs=[
                pl.BlockSpec((1, span, local_cols), lambda b, s, _: (b, 0, 0)),
                pl.BlockSpec((2, 1, prefix_cap, HD), lambda b, s, _: (0, b, 0, s[0])),
                pl.BlockSpec((2, 1, span, HD), lambda b, s, _: (0, b, 0, s[0])),
            ],
            out_specs=pl.BlockSpec(
                (2, 2, z_count // seqs, rows, local_cols), lambda b, s, _: (0, 0, b, 0, 0)
            ),
        ),
        out_shape=jax.ShapeDtypeStruct((2, 2, z_count, rows, local_cols), bf16),
        compiler_params=pltpu.CompilerParams(vmem_limit_bytes=60 * MIB),
    )(
        kv_head[None].astype(jnp.int32), prefix_len,
        queries, kv_cache, span_kv,
    )

    chunks = width // CHUNK
    vmem = pl.BlockSpec(memory_space=pltpu.VMEM)
    hbm = pl.BlockSpec(memory_space=pl.ANY)
    one = pltpu.SemaphoreType.DMA((chunks,))
    per_far = pltpu.SemaphoreType.DMA((chunks, far_count))
    gathered = pl.pallas_call(
        exchange_kernel,
        out_shape=jax.ShapeDtypeStruct((far_count, 2, 2, 2, rows, width), bf16),
        in_specs=[vmem, hbm, vmem, vmem],
        out_specs=hbm,
        scratch_shapes=[
            pltpu.VMEM((chunks, local_cols, CHUNK), bf16),
            pltpu.VMEM((chunks, 2, 2, far_count, 2, rows, CHUNK), bf16),
            pltpu.VMEM((chunks, 2, far_count, 2, rows, CHUNK), bf16),
            pltpu.VMEM((chunks, far_count, 2, rows, CHUNK), bf16),
            pltpu.VMEM((chunks, 2, far_count, rows, CHUNK), bf16),
            pltpu.VMEM((chunks, far_count, rows, CHUNK), bf16),
            pltpu.VMEM((chunks, far_count, rows, CHUNK), bf16),
            pltpu.VMEM((chunks, rows, CHUNK), bf16),
            pltpu.VMEM((HB, HB), jnp.float32),
            one, one, one, one, one, one, one, one, per_far, per_far,
            per_far, per_far, one, one, one, one, one, one,
        ],
        compiler_params=pltpu.CompilerParams(
            collective_id=0, has_side_effects=True, vmem_limit_bytes=56 * MIB
        ),
    )(
        attended.reshape(n * rows, local_cols), out_weight, residual, sign_bits[None],
    )
    gathered = gathered.reshape(n * rows, width)

    stream, normed = pl.pallas_call(
        norm_kernel,
        grid_spec=pltpu.PrefetchScalarGridSpec(
            num_scalar_prefetch=1,
            grid=(n * rows // NORM_ROWS,),
            in_specs=[pl.BlockSpec((NORM_ROWS, width), lambda i, s: (i, 0))],
            out_specs=[
                pl.BlockSpec((rows, width), lambda i, s: (0, 0)),
                pl.BlockSpec((NORM_ROWS, width), lambda i, s: (i, 0)),
            ],
        ),
        out_shape=[
            jax.ShapeDtypeStruct((rows, width), bf16),
            jax.ShapeDtypeStruct((n * rows, width), bf16),
        ],
        compiler_params=pltpu.CompilerParams(vmem_limit_bytes=60 * MIB),
    )(me[None].astype(jnp.int32), gathered)
    return (stream, normed)


def solution(mesh):
    in_specs = (
        P("grp", None, "tp"),
        P(None, "grp", None, None),
        P(None, "grp", None, None),
        P("grp"),
        P(("grp", "tp"), None),
        P("tp", None),
        P(),
    )
    out_specs = (P(("grp", "tp"), None), P("grp", None))
    return jax.shard_map(
        functools.partial(body, mesh.shape["tp"]),
        mesh=mesh, in_specs=in_specs, out_specs=out_specs, check_vma=False,
    )
```
